1024 devices in a mesh: face: 128 (over z, y), tile: 8 (over x, core).
Axes of the slice: x: 4, y: 8, z: 16, core: 2. Of those that a mesh axis runs over, the one named last changes fastest.
Arguments:
- model_field: bfloat16 [2097152, 128], P(('face', 'tile')), may hold values from -6 to 6
- interp_weight: bfloat16 [262144, 2048], P(('face', 'tile')), may hold values from -0.125 to 0.125
- center_block: bfloat16 [262144, 256], P(('face', 'tile')), may hold values from -0.21875 to 0.21875
- lower_block: bfloat16 [262144, 256], P(('face', 'tile')), may hold values from -0.21875 to 0.21875
- upper_block: bfloat16 [262144, 256], P(('face', 'tile')), may hold values from -0.21875 to 0.21875
- owner_slots: int32 [1024, 256], P(('face', 'tile')), may hold values from 0 to 255, each once within a row
Outputs:
- localized: bfloat16 [2097152, 128], P(('face', 'tile'))
The draws below stay inside these ranges and needn't reach their ends.
Inputs may be any that keep to these rules, and one draw needn't show every extreme that they name: `owner_slots`: each row is a permutation of 0 to 255.
All inputs are finite; a program needn't handle non-finite values.
Results may differ from the reference program's by a relative error of at most 0.013.
Values may be sent and summed in bfloat16 or wider, within the bound.
A program may use at most 32 MiB of HBM per device.

```python
import jax
import jax.numpy as jnp
from jax import lax

K = 128
M = 2048
P_SIZE = 256
TILES = 1024
N_FACE = 128
N_TILE = 8


def levels(own_key, extent, cuts, least, high):
    level = 1.0
    for dim, shards_of in cuts:
        draws = jax.random.uniform(jax.random.fold_in(jax.random.fold_in(own_key, 6), dim), (shards_of,), jnp.float32, least / len(cuts), high / len(cuts))
        level = level * jnp.repeat(jnp.exp(draws), extent[dim] // shards_of).reshape((-1,) + (1,) * (len(extent) - 1 - dim))
    return level


def gaussian(rng, shape, width, most, cuts=(), held_as=jnp.bfloat16):
    entries = jax.random.normal(rng, shape, jnp.float32) * width
    if len(cuts) > 0:
        entries = levels(rng, shape, cuts, -0.22, 0.18) * entries
    return jnp.clip(entries, min=-most, max=most).astype(held_as)


def setup_inputs(seed: int = 0) -> dict:
    key_of = jax.random.split(jax.random.key(seed), 7)
    return {
        "model_field": gaussian(key_of[0], (TILES * M, K), 1.0, 6.0, ((0, 1024),)),
        "interp_weight": gaussian(key_of[1], (TILES * P_SIZE, M), M ** -0.5, 0.125, ((0, 1024),)),
        "center_block": gaussian(key_of[2], (TILES * P_SIZE, P_SIZE), (3 * P_SIZE) ** -0.5, 0.21875, ((0, 1024),)),
        "lower_block": gaussian(key_of[3], (TILES * P_SIZE, P_SIZE), (3 * P_SIZE) ** -0.5, 0.21875, ((0, 1024),)),
        "upper_block": gaussian(key_of[4], (TILES * P_SIZE, P_SIZE), (3 * P_SIZE) ** -0.5, 0.21875, ((0, 1024),)),
        "owner_slots": jax.vmap(lambda own: jax.random.permutation(own, P_SIZE))(jax.random.split(key_of[5], TILES)).reshape((TILES, P_SIZE)).astype(jnp.int32),
    }


def reference(model_field, interp_weight, center_block, lower_block, upper_block, owner_slots):
    share = P_SIZE // N_FACE
    fields = model_field.reshape(TILES, M, K)
    weights = interp_weight.reshape(TILES, P_SIZE, M)
    center = center_block.reshape(TILES, P_SIZE, P_SIZE)
    lower = lower_block.reshape(TILES, P_SIZE, P_SIZE)
    upper = upper_block.reshape(TILES, P_SIZE, P_SIZE)

    def interp_one(pair):
        return jnp.dot(pair[0], pair[1], preferred_element_type=jnp.float32).astype(jnp.bfloat16)

    subset = lax.map(interp_one, (weights, fields))
    slotted = jnp.take_along_axis(subset, owner_slots[:, :, None], axis=1)
    slotted = slotted.reshape(N_FACE, N_TILE, N_FACE, share, K)
    owned = jnp.transpose(slotted, (2, 1, 0, 3, 4)).reshape(N_FACE, N_TILE, P_SIZE, K)
    below = jnp.roll(owned, 1, axis=1).reshape(TILES, P_SIZE, K)
    above = jnp.roll(owned, -1, axis=1).reshape(TILES, P_SIZE, K)
    owned = owned.reshape(TILES, P_SIZE, K)

    def conv_one(items):
        a, l, r, v, vb, va = items
        total = jnp.dot(a, v, preferred_element_type=jnp.float32)
        total = total + jnp.dot(l, vb, preferred_element_type=jnp.float32)
        total = total + jnp.dot(r, va, preferred_element_type=jnp.float32)
        return total.astype(jnp.bfloat16)

    conv = lax.map(conv_one, (center, lower, upper, owned, below, above))

    def adj_one(items):
        a, l, r, w = items
        own = jnp.dot(a.T, w, preferred_element_type=jnp.float32)
        low = jnp.dot(l.T, w, preferred_element_type=jnp.float32)
        upp = jnp.dot(r.T, w, preferred_element_type=jnp.float32)
        return own, low, upp

    own_term, low_term, upp_term = lax.map(adj_one, (center, lower, upper, conv))
    low_term = jnp.roll(low_term.reshape(N_FACE, N_TILE, P_SIZE, K), -1, axis=1).reshape(TILES, P_SIZE, K)
    upp_term = jnp.roll(upp_term.reshape(N_FACE, N_TILE, P_SIZE, K), 1, axis=1).reshape(TILES, P_SIZE, K)
    adjoint = (own_term + low_term + upp_term).astype(jnp.bfloat16)
    returned = adjoint.reshape(N_FACE, N_TILE, N_FACE, share, K)
    returned = jnp.transpose(returned, (2, 1, 0, 3, 4)).reshape(TILES, P_SIZE, K)

    def place_one(pair):
        return jnp.zeros((P_SIZE, K), jnp.bfloat16).at[pair[0]].set(pair[1])

    back = lax.map(place_one, (owner_slots, returned))

    def out_one(pair):
        return jnp.dot(pair[0].T, pair[1], preferred_element_type=jnp.float32).astype(jnp.bfloat16)

    localized = lax.map(out_one, (weights, back))
    return localized.reshape(TILES * M, K)
```

```python
import functools

import jax
import jax.numpy as jnp
from jax import lax
from jax.experimental import pallas as pl
from jax.experimental.pallas import tpu as pltpu
from jax.sharding import PartitionSpec as P

MESH = pl.DeviceIdType.MESH
F32, BF16 = jnp.float32, jnp.bfloat16
CHUNKS = 4


def dot(a, b, ca=1, cb=0):
    return lax.dot_general(a, b, (((ca,), (cb,)), ((), ())), preferred_element_type=F32)


def far_first(size):
    order = [size // 2] if size % 2 == 0 else []
    for d in range((size - 1) // 2, 0, -1):
        order += [d, size - d]
    return order


def kernel(
    ny, nz, nt,
    x_hbm, w_hbm, a_hbm, l_hbm, r_hbm, s_hbm, out_hbm,
    x_v, w_v, a_v, l_v, r_v, s_v, g_v, out_v,
    perm_v, swap_v, unswap_v,
    send1, recv1, send2, owned, below, above, low_out, upp_out, low_in, upp_in,
    send3, recv3, send4, recv4,
    load_sem, out_sem, send_sem, recv_sem,
):
    face, tile = lax.axis_index("face"), lax.axis_index("tile")
    z, y = lax.div(face, ny), lax.rem(face, ny)
    points, width = owned.shape
    share = points // (ny * nz)
    yrows, zrows = nz * share, ny * share
    depth = w_v.shape[1] // CHUNKS
    prev, nxt = lax.rem(tile + nt - 1, nt), lax.rem(tile + 1, nt)
    y_mates = [lax.rem(y + d, ny) for d in far_first(ny)]
    z_mates = [lax.rem(z + d, nz) for d in far_first(nz)]

    barrier = pltpu.get_barrier_semaphore()
    for m in z_mates:
        pl.semaphore_signal(barrier, inc=1, device_id={"face": m * ny + y}, device_id_type=MESH)
    for m in y_mates:
        pl.semaphore_signal(barrier, inc=1, device_id={"face": z * ny + m}, device_id_type=MESH)
    for m in (prev, nxt):
        pl.semaphore_signal(barrier, inc=1, device_id={"tile": m}, device_id_type=MESH)

    loads = [pltpu.make_async_copy(s_hbm, s_v, load_sem.at[0])]
    for c in range(CHUNKS):
        span = pl.ds(c * depth, depth)
        loads.append(pltpu.make_async_copy(x_hbm.at[span], x_v.at[span], load_sem.at[1 + 2 * c]))
        loads.append(pltpu.make_async_copy(w_hbm.at[:, span], w_v.at[:, span], load_sem.at[2 + 2 * c]))
    for i, (src, dst) in enumerate(((a_hbm, a_v), (l_hbm, l_v), (r_hbm, r_v))):
        loads.append(pltpu.make_async_copy(src, dst, load_sem.at[1 + 2 * CHUNKS + i]))
    for load in loads:
        load.start()

    rows = lax.broadcasted_iota(jnp.int32, (points, points), 0)
    cols = lax.broadcasted_iota(jnp.int32, (points, points), 1)

    def y_major(i):
        f, q = lax.div(i, share), lax.rem(i, share)
        return (lax.rem(f, ny) * nz + lax.div(f, ny)) * share + q

    swap_v[...] = jnp.where(cols == y_major(rows), 1.0, 0.0).astype(BF16)
    unswap_v[...] = jnp.where(rows == y_major(cols), 1.0, 0.0).astype(BF16)
    loads[0].wait()
    slots = jnp.broadcast_to(s_v[...].astype(F32), (points, points)).astype(BF16)
    slots = dot(unswap_v[...], slots, 1, 1)
    perm_v[...] = jnp.where(slots == cols.astype(F32), 1.0, 0.0).astype(BF16)

    total = None
    for c in range(CHUNKS):
        span = pl.ds(c * depth, depth)
        loads[1 + 2 * c].wait()
        loads[2 + 2 * c].wait()
        term = dot(w_v[:, span], x_v[span, :])
        total = term if total is None else total + term
    send1[...] = dot(perm_v[...], total.astype(BF16)).astype(BF16)

    pl.semaphore_wait(barrier, len(z_mates) + len(y_mates) + 2)

    def to_mates(phase, mates, face_of, mine, src, dst, size):
        here = pl.ds(pl.multiple_of(mine * size, size), size)
        copies = []
        for m in mates:
            copies.append(pltpu.make_async_remote_copy(
                src_ref=src.at[pl.ds(pl.multiple_of(m * size, size), size)],
                dst_ref=dst.at[here],
                send_sem=send_sem.at[phase],
                recv_sem=recv_sem.at[phase],
                device_id={"face": face_of(m)},
                device_id_type=MESH,
            ))
        for copy in copies:
            copy.start()
        dst[here, :] = src[here, :]
        span = pl.ds(0, size * len(mates))
        return pltpu.make_async_remote_copy(
            src_ref=src.at[span], dst_ref=dst.at[span],
            send_sem=send_sem.at[phase], recv_sem=recv_sem.at[phase],
            device_id={"face": face_of(mates[0])}, device_id_type=MESH,
        )

    def to_tile(phase, other, src, dst):
        copy = pltpu.make_async_remote_copy(
            src_ref=src, dst_ref=dst, send_sem=send_sem.at[phase], recv_sem=recv_sem.at[phase],
            device_id={"tile": other}, device_id_type=MESH,
        )
        copy.start()
        return copy

    waits = []
    waits.append(to_mates(0, y_mates, lambda m: z * ny + m, y, send1, recv1, yrows))
    for load in loads[1 + 2 * CHUNKS:]:
        load.wait()
    waits[-1].wait_recv()
    send2[...] = dot(swap_v[...], recv1[...]).astype(BF16)
    waits.append(to_mates(1, z_mates, lambda m: m * ny + y, z, send2, owned, zrows))
    for c in range(CHUNKS):
        span = pl.ds(c * depth, depth)
        g_v[span, :] = dot(w_v[:, span], perm_v[...], 0, 1).astype(BF16)
    waits[-1].wait_recv()

    waits.append(to_tile(2, nxt, owned, below))
    waits.append(to_tile(3, prev, owned, above))
    conv = dot(a_v[...], owned[...])
    waits[2].wait_recv()
    conv = conv + dot(l_v[...], below[...])
    waits[3].wait_recv()
    conv = (conv + dot(r_v[...], above[...])).astype(BF16)
    low_out[...] = dot(l_v[...], conv, 0, 0).astype(BF16)
    waits.append(to_tile(4, prev, low_out, low_in))
    upp_out[...] = dot(r_v[...], conv, 0, 0).astype(BF16)
    waits.append(to_tile(5, nxt, upp_out, upp_in))
    adjoint = dot(a_v[...], conv, 0, 0)
    waits[4].wait_recv()
    adjoint = adjoint + low_in[...].astype(F32)
    waits[5].wait_recv()
    send3[...] = (adjoint + upp_in[...].astype(F32)).astype(BF16)

    waits.append(to_mates(6, z_mates, lambda m: m * ny + y, z, send3, recv3, zrows))
    waits[-1].wait_recv()
    send4[...] = dot(unswap_v[...], recv3[...]).astype(BF16)
    waits.append(to_mates(7, y_mates, lambda m: z * ny + m, y, send4, recv4, yrows))
    waits[-1].wait_recv()

    stores = []
    for c in range(CHUNKS):
        span = pl.ds(c * depth, depth)
        out_v[span, :] = dot(g_v[span, :], recv4[...]).astype(BF16)
        stores.append(pltpu.make_async_copy(out_v.at[span], out_hbm.at[span], out_sem.at[c]))
        stores[-1].start()
    for wait in waits:
        wait.wait_send()
    for store in stores:
        store.wait()


def solution(mesh):
    nf, nt = mesh.shape["face"], mesh.shape["tile"]
    ny = 8 if nf == 128 else 2
    nz = nf // ny

    def local(model_field, interp_weight, center_block, lower_block, upper_block, owner_slots):
        model, width = model_field.shape
        points = interp_weight.shape[0]
        field = pltpu.VMEM((points, width), BF16)
        block = pltpu.VMEM((points, points), BF16)
        return pl.pallas_call(
            functools.partial(kernel, ny, nz, nt),
            out_shape=jax.ShapeDtypeStruct((model, width), BF16),
            in_specs=[pl.BlockSpec(memory_space=pl.ANY)] * 6,
            out_specs=pl.BlockSpec(memory_space=pl.ANY),
            scratch_shapes=[
                pltpu.VMEM((model, width), BF16),
                pltpu.VMEM((points, model), BF16),
                block, block, block,
                pltpu.VMEM((1, points), jnp.int32),
                pltpu.VMEM((model, points), BF16),
                pltpu.VMEM((model, width), BF16),
                block, block, block,
            ] + [field] * 14 + [
                pltpu.SemaphoreType.DMA((4 + 2 * CHUNKS,)),
                pltpu.SemaphoreType.DMA((CHUNKS,)),
                pltpu.SemaphoreType.DMA((8,)),
                pltpu.SemaphoreType.DMA((8,)),
            ],
            compiler_params=pltpu.CompilerParams(
                collective_id=0, has_side_effects=True, vmem_limit_bytes=24 * 2**20
            ),
            cost_estimate=pl.CostEstimate(
                flops=6 * points * model * width, bytes_accessed=6 * model * points, transcendentals=0
            ),
        )(model_field, interp_weight, center_block, lower_block, upper_block, owner_slots)

    placed = P(("face", "tile"), None)
    return jax.shard_map(
        local, mesh=mesh, in_specs=(placed,) * 6, out_specs=placed, check_vma=False
    )
```

```python
import functools

import jax
import jax.numpy as jnp
from jax import lax
from jax.experimental import pallas as pl
from jax.experimental.pallas import tpu as pltpu
from jax.sharding import PartitionSpec as P

MESH = pl.DeviceIdType.MESH
F32, BF16 = jnp.float32, jnp.bfloat16
CHUNKS = 4
OTHERS = (1, -1, 2, -2)


def dot(a, b, ca=1, cb=0):
    return lax.dot_general(a, b, (((ca,), (cb,)), ((), ())), preferred_element_type=F32)


def away(k, size):
    half = lax.div(k + 1, 2)
    return size // 2 + jnp.where(lax.rem(k, 2) == 1, -half, half)


def kernel(
    ny, nz, nt,
    x_hbm, w_hbm, a_hbm, l_hbm, r_hbm, s_hbm, back, w_v,
    x_v, s_v, perm_v, blocks, near, mixed,
    send1, owned3, owned, around, send2, recv2,
    load_sem, send_sem, recv_sem,
):
    face, tile = lax.axis_index("face"), lax.axis_index("tile")
    z, y = lax.div(face, ny), lax.rem(face, ny)
    faces, share, width = owned3.shape
    points = faces * share
    depth = w_v.shape[1] // CHUNKS

    def beside(d):
        return lax.rem(tile + nt + d, nt)

    def to_each_mate(act):
        def step(i, carry):
            dz, dy = away(lax.div(i, ny), nz), away(lax.rem(i, ny), ny)
            act(lax.rem(z + dz, nz) * ny + lax.rem(y + dy, ny))
            return carry

        lax.fori_loop(0, faces - 1, step, 0)

    barrier = pltpu.get_barrier_semaphore()
    to_each_mate(lambda m: pl.semaphore_signal(barrier, inc=1, device_id={"face": m}, device_id_type=MESH))
    for d in OTHERS:
        pl.semaphore_signal(barrier, inc=1, device_id={"tile": beside(d)}, device_id_type=MESH)

    def load(c):
        span = pl.ds(pl.multiple_of(c * depth, depth), depth)
        return (
            pltpu.make_async_copy(x_hbm.at[span], x_v.at[span], load_sem.at[2 * c]),
            pltpu.make_async_copy(w_hbm.at[:, span], w_v.at[:, span], load_sem.at[2 * c + 1]),
        )

    for c in range(CHUNKS):
        for copy in load(c):
            copy.start()
    loads = []
    for i, (src, dst) in enumerate(((s_hbm, s_v), (a_hbm, blocks.at[0]), (l_hbm, blocks.at[1]), (r_hbm, blocks.at[2]))):
        loads.append(pltpu.make_async_copy(src, dst, load_sem.at[2 * CHUNKS + i]))
        loads[-1].start()

    def add(c, total):
        span = pl.ds(pl.multiple_of(c * depth, depth), depth)
        for copy in load(c):
            copy.wait()
        return total + dot(w_v[:, span], x_v[span, :])

    total = lax.fori_loop(0, CHUNKS, add, jnp.zeros((points, width), F32))
    loads[0].wait()
    rows = lax.broadcasted_iota(jnp.int32, (points, points), 0)
    perm_v[...] = jnp.where(rows == s_v[...], 1.0, 0.0).astype(BF16)
    send1[...] = dot(perm_v[...], total.astype(BF16), 0, 0).astype(BF16).reshape(faces, share, width)
    for copy in loads[1:]:
        copy.wait()

    pl.semaphore_wait(barrier, faces - 1 + len(OTHERS))

    def to_mates(phase, src, dst):
        to_each_mate(lambda m: pltpu.make_async_remote_copy(
            src_ref=src.at[m], dst_ref=dst.at[face],
            send_sem=send_sem.at[phase], recv_sem=recv_sem.at[phase],
            device_id={"face": m}, device_id_type=MESH,
        ).start())
        dst[face] = src[face]
        span = pl.ds(0, faces - 1)
        return pltpu.make_async_remote_copy(
            src_ref=src.at[span], dst_ref=dst.at[span],
            send_sem=send_sem.at[phase], recv_sem=recv_sem.at[phase],
            device_id={"face": lax.rem(face + 1, faces)}, device_id_type=MESH,
        )

    def to_tile(phase, other, src, dst):
        copy = pltpu.make_async_remote_copy(
            src_ref=src, dst_ref=dst, send_sem=send_sem.at[phase], recv_sem=recv_sem.at[phase],
            device_id={"tile": other}, device_id_type=MESH,
        )
        copy.start()
        return copy

    waits = []
    waits.append(to_mates(0, send1, owned3))
    waits.append(to_tile(1, beside(-1), blocks, near.at[1]))
    waits.append(to_tile(2, beside(1), blocks, near.at[0]))
    waits[0].wait_recv()
    owned[...] = owned3[...].reshape(points, width)

    fields = [to_tile(3 + k, beside(-OTHERS[k]), owned, around.at[k]) for k in (2, 3, 0, 1)]
    waits += fields
    waits[1].wait_recv()
    waits[2].wait_recv()

    a, l, r = (blocks[i] for i in range(3))
    ap, lp, rp = (near[0, i] for i in range(3))
    an, ln, rn = (near[1, i] for i in range(3))
    mixed[0] = (dot(a, a, 0, 0) + dot(ln, ln, 0, 0) + dot(rp, rp, 0, 0)).astype(BF16)
    mixed[1] = (dot(a, r, 0, 0) + dot(ln, an, 0, 0)).astype(BF16)
    mixed[2] = (dot(a, l, 0, 0) + dot(rp, ap, 0, 0)).astype(BF16)
    mixed[3] = dot(ln, rn, 0, 0).astype(BF16)
    mixed[4] = dot(rp, lp, 0, 0).astype(BF16)
    adjoint = dot(mixed[0], owned[...])
    for k, field in ((0, fields[2]), (1, fields[3]), (2, fields[0]), (3, fields[1])):
        field.wait_recv()
        adjoint = adjoint + dot(mixed[1 + k], around[k])
    send2[...] = adjoint.astype(BF16).reshape(faces, share, width)

    waits.append(to_mates(7, send2, recv2))
    waits[-1].wait_recv()
    back[...] = dot(perm_v[...], recv2[...].reshape(points, width)).astype(BF16)
    for wait in waits:
        wait.wait_send()


def spread(w_ref, back_ref, out_hbm, out_v, out_sem):
    depth = w_ref.shape[1] // CHUNKS

    stores = []
    for c in range(CHUNKS):
        span = pl.ds(c * depth, depth)
        out_v[span, :] = dot(w_ref[:, span], back_ref[...], 0, 0).astype(BF16)
        stores.append(pltpu.make_async_copy(out_v.at[span], out_hbm.at[span], out_sem.at[c]))
        stores[-1].start()
    for store in stores:
        store.wait()


def solution(mesh):
    nf, nt = mesh.shape["face"], mesh.shape["tile"]
    ny = 8 if nf == 128 else 2
    nz = nf // ny

    def local(model_field, interp_weight, center_block, lower_block, upper_block, owner_slots):
        model, width = model_field.shape
        points = interp_weight.shape[0]
        field = pltpu.VMEM((points, width), BF16)
        field3 = pltpu.VMEM((nf, points // nf, width), BF16)
        back, weight = pl.pallas_call(
            functools.partial(kernel, ny, nz, nt),
            out_shape=(
                jax.ShapeDtypeStruct((points, width), BF16),
                jax.ShapeDtypeStruct((points, model), BF16),
            ),
            in_specs=[pl.BlockSpec(memory_space=pltpu.HBM)] * 6,
            out_specs=[pl.BlockSpec(memory_space=pltpu.VMEM)] * 2,
            scratch_shapes=[
                pltpu.VMEM((model, width), BF16),
                pltpu.VMEM((1, points), jnp.int32),
                pltpu.VMEM((points, points), BF16),
                pltpu.VMEM((3, points, points), BF16),
                pltpu.VMEM((2, 3, points, points), BF16),
                pltpu.VMEM((5, points, points), BF16),
                field3, field3, field, pltpu.VMEM((4, points, width), BF16), field3, field3,
                pltpu.SemaphoreType.DMA((4 + 2 * CHUNKS,)),
                pltpu.SemaphoreType.DMA((8,)),
                pltpu.SemaphoreType.DMA((8,)),
            ],
            compiler_params=pltpu.CompilerParams(
                collective_id=0, has_side_effects=True, vmem_limit_bytes=16 * 2**20
            ),
            cost_estimate=pl.CostEstimate(
                flops=6 * points * model * width, bytes_accessed=6 * model * points, transcendentals=0
            ),
        )(*(pltpu.with_memory_space_constraint(v, pltpu.HBM) for v in (
            model_field, interp_weight, center_block, lower_block, upper_block, owner_slots
        )))
        return pl.pallas_call(
            spread,
            out_shape=jax.ShapeDtypeStruct((model, width), BF16),
            in_specs=[pl.BlockSpec(memory_space=pltpu.VMEM)] * 2,
            out_specs=pl.BlockSpec(memory_space=pltpu.HBM),
            scratch_shapes=[pltpu.VMEM((model, width), BF16), pltpu.SemaphoreType.DMA((CHUNKS,))],
            compiler_params=pltpu.CompilerParams(vmem_limit_bytes=16 * 2**20),
            cost_estimate=pl.CostEstimate(
                flops=2 * points * model * width, bytes_accessed=4 * model * points, transcendentals=0
            ),
        )(weight, back)

    placed = P(("face", "tile"), None)
    return jax.shard_map(
        local, mesh=mesh, in_specs=(placed,) * 6, out_specs=placed, check_vma=False
    )
```

```python
import functools

import jax
import jax.numpy as jnp
from jax import lax
from jax.experimental import pallas as pl
from jax.experimental.pallas import tpu as pltpu
from jax.sharding import PartitionSpec as P

MESH = pl.DeviceIdType.MESH
F32, BF16 = jnp.float32, jnp.bfloat16
LOADS = 2
STORES = 4
OTHERS = (1, -1, 2, -2)


def dot(a, b, ca=1, cb=0):
    return lax.dot_general(a, b, (((ca,), (cb,)), ((), ())), preferred_element_type=F32)


def away(k, size):
    half = lax.div(k + 1, 2)
    return size // 2 + jnp.where(lax.rem(k, 2) == 1, -half, half)


def kernel(
    ny, nz, nt,
    x_hbm, w_hbm, a_hbm, l_hbm, r_hbm, s_hbm, returned, weight,
    x_v, w_v, s_v, perm_v, blocks, near, mixed,
    send1, owned, around, send2, recv2,
    load_sem, send_sem, recv_sem,
):
    face, tile = lax.axis_index("face"), lax.axis_index("tile")
    z, y = lax.div(face, ny), lax.rem(face, ny)
    faces, share, width = owned.shape
    points = faces * share
    depth = w_v.shape[1] // LOADS
    far = max(1, nz * 7 // 16)

    def beside(d):
        return lax.rem(tile + nt + d, nt)

    def plane(k):
        return lax.rem(z + away(k, nz), nz)

    def to_mates(act, first=0, last=faces - 1):
        def step(i, carry):
            act(plane(lax.div(i, ny)) * ny + lax.rem(y + away(lax.rem(i, ny), ny), ny))
            return carry

        lax.fori_loop(first, last, step, 0)

    loads = []
    for c in range(LOADS):
        span = pl.ds(c * depth, depth)
        loads.append(pltpu.make_async_copy(x_hbm.at[span], x_v.at[span], load_sem.at[2 * c]))
        loads.append(pltpu.make_async_copy(w_hbm.at[:, span], w_v.at[:, span], load_sem.at[2 * c + 1]))
    for copy in loads:
        copy.start()

    barrier = pltpu.get_barrier_semaphore()
    to_mates(lambda m: pl.semaphore_signal(barrier, inc=1, device_id={"face": m}, device_id_type=MESH))
    for d in OTHERS:
        pl.semaphore_signal(barrier, inc=1, device_id={"tile": beside(d)}, device_id_type=MESH)

    for i, (src, dst) in enumerate((
        (s_hbm, s_v), (a_hbm, blocks.at[0]), (l_hbm, blocks.at[1]), (r_hbm, blocks.at[2])
    )):
        loads.append(pltpu.make_async_copy(src, dst, load_sem.at[2 * LOADS + i]))
        loads[-1].start()

    total = None
    for c in range(LOADS):
        span = pl.ds(c * depth, depth)
        loads[2 * c].wait()
        loads[2 * c + 1].wait()
        term = dot(w_v[:, span], x_v[span, :])
        total = term if total is None else total + term
    loads[2 * LOADS].wait()
    rows = lax.broadcasted_iota(jnp.int32, (points, points), 0)
    perm_v[...] = jnp.where(rows == s_v[...], 1.0, 0.0).astype(BF16)
    send1[...] = dot(perm_v[...], total.astype(BF16), 0, 0).astype(BF16).reshape(faces, share, width)
    owned[face] = send1[face]
    for copy in loads[2 * LOADS + 1:]:
        copy.wait()

    pl.semaphore_wait(barrier, faces - 1 + len(OTHERS))

    def remote(src, dst, phase, other):
        return pltpu.make_async_remote_copy(
            src_ref=src, dst_ref=dst, send_sem=send_sem.at[phase], recv_sem=recv_sem.at[phase],
            device_id=other, device_id_type=MESH,
        )

    def exchange(phase, src, dst, first, last):
        to_mates(lambda m: remote(src.at[m], dst.at[face], phase, {"face": m}).start(), first, last)
        span = pl.ds(0, last - first)
        return remote(src.at[span], dst.at[span], phase, {"face": lax.rem(face + 1, faces)})

    far_half = exchange(0, send1, owned, 0, far * ny)
    near_half = exchange(1, send1, owned, far * ny, faces - 1)
    to_prev = remote(blocks, near.at[1], 2, {"tile": beside(-1)})
    to_next = remote(blocks, near.at[0], 3, {"tile": beside(1)})
    to_prev.start()
    to_next.start()
    waits = [far_half, near_half, to_prev, to_next]
    weight[...] = dot(w_v[...], perm_v[...], 0, 0).astype(BF16)

    def hand_on(first, last):
        def step(k, carry):
            span = pl.ds(plane(k) * ny, ny)
            for j in (2, 3, 0, 1):
                remote(owned.at[span], around.at[j, span], 4 + j, {"tile": beside(-OTHERS[j])}).start()
            return carry

        lax.fori_loop(first, last, step, 0)

    near_half.wait_recv()
    hand_on(far, nz)
    far_half.wait_recv()
    hand_on(0, far)
    fields = [remote(owned, around.at[j], 4 + j, {"tile": beside(-d)}) for j, d in enumerate(OTHERS)]
    waits += fields

    to_prev.wait_recv()
    to_next.wait_recv()
    a, l, r = (blocks[i] for i in range(3))
    ap, lp, rp = (near[0, i] for i in range(3))
    an, ln, rn = (near[1, i] for i in range(3))
    mixed[0] = (dot(a, a, 0, 0) + dot(ln, ln, 0, 0) + dot(rp, rp, 0, 0)).astype(BF16)
    mixed[1] = (dot(a, r, 0, 0) + dot(ln, an, 0, 0)).astype(BF16)
    mixed[2] = (dot(a, l, 0, 0) + dot(rp, ap, 0, 0)).astype(BF16)
    mixed[3] = dot(ln, rn, 0, 0).astype(BF16)
    mixed[4] = dot(rp, lp, 0, 0).astype(BF16)
    adjoint = dot(mixed[0], owned[...].reshape(points, width))
    for j, field in enumerate(fields):
        field.wait_recv()
        adjoint = adjoint + dot(mixed[1 + j], around[j].reshape(points, width))
    send2[...] = adjoint.astype(BF16).reshape(faces, share, width)

    waits.append(exchange(8, send2, recv2, 0, faces - 1))
    recv2[face] = send2[face]
    waits[-1].wait_recv()
    returned[...] = recv2[...].reshape(points, width)
    for wait in waits:
        wait.wait_send()


def spread(weight_ref, returned_ref, out_hbm, out_v, out_sem):
    depth = weight_ref.shape[0] // STORES
    stores = []
    for c in range(STORES):
        span = pl.ds(c * depth, depth)
        out_v[span, :] = dot(weight_ref[span, :], returned_ref[...]).astype(BF16)
        stores.append(pltpu.make_async_copy(out_v.at[span], out_hbm.at[span], out_sem.at[c]))
        stores[-1].start()
    for store in stores:
        store.wait()


def solution(mesh):
    nf, nt = mesh.shape["face"], mesh.shape["tile"]
    ny = 8 if nf == 128 else 2
    nz = nf // ny

    def local(model_field, interp_weight, center_block, lower_block, upper_block, owner_slots):
        model, width = model_field.shape
        points = interp_weight.shape[0]
        field = pltpu.VMEM((nf, points // nf, width), BF16)
        returned, weight = pl.pallas_call(
            functools.partial(kernel, ny, nz, nt),
            out_shape=(
                jax.ShapeDtypeStruct((points, width), BF16),
                jax.ShapeDtypeStruct((model, points), BF16),
            ),
            in_specs=[pl.BlockSpec(memory_space=pltpu.HBM)] * 6,
            out_specs=[pl.BlockSpec(memory_space=pltpu.VMEM)] * 2,
            scratch_shapes=[
                pltpu.VMEM((model, width), BF16),
                pltpu.VMEM((points, model), BF16),
                pltpu.VMEM((1, points), jnp.int32),
                pltpu.VMEM((points, points), BF16),
                pltpu.VMEM((3, points, points), BF16),
                pltpu.VMEM((2, 3, points, points), BF16),
                pltpu.VMEM((5, points, points), BF16),
                field, field, pltpu.VMEM((4, nf, points // nf, width), BF16), field, field,
                pltpu.SemaphoreType.DMA((4 + 2 * LOADS,)),
                pltpu.SemaphoreType.DMA((9,)),
                pltpu.SemaphoreType.DMA((9,)),
            ],
            compiler_params=pltpu.CompilerParams(
                collective_id=0, has_side_effects=True, vmem_limit_bytes=16 * 2**20
            ),
            cost_estimate=pl.CostEstimate(
                flops=6 * points * model * width, bytes_accessed=6 * model * points, transcendentals=0
            ),
        )(*(pltpu.with_memory_space_constraint(v, pltpu.HBM) for v in (
            model_field, interp_weight, center_block, lower_block, upper_block, owner_slots
        )))
        return pl.pallas_call(
            spread,
            out_shape=jax.ShapeDtypeStruct((model, width), BF16),
            in_specs=[pl.BlockSpec(memory_space=pltpu.VMEM)] * 2,
            out_specs=pl.BlockSpec(memory_space=pltpu.HBM),
            scratch_shapes=[pltpu.VMEM((model, width), BF16), pltpu.SemaphoreType.DMA((STORES,))],
            compiler_params=pltpu.CompilerParams(vmem_limit_bytes=16 * 2**20),
            cost_estimate=pl.CostEstimate(
                flops=2 * points * model * width, bytes_accessed=4 * model * points, transcendentals=0
            ),
        )(weight, returned)

    placed = P(("face", "tile"), None)
    return jax.shard_map(
        local, mesh=mesh, in_specs=(placed,) * 6, out_specs=placed, check_vma=False
    )
```

```python
import functools

import jax
import jax.numpy as jnp
from jax import lax
from jax.experimental import pallas as pl
from jax.experimental.pallas import tpu as pltpu
from jax.sharding import PartitionSpec as P

MESH = pl.DeviceIdType.MESH
F32, BF16 = jnp.float32, jnp.bfloat16
LOADS = 2
STORES = 4
OTHERS = (1, -1, 2, -2)


def dot(a, b, ca=1, cb=0):
    return lax.dot_general(a, b, (((ca,), (cb,)), ((), ())), preferred_element_type=F32)


def away(k, size):
    half = lax.div(k + 1, 2)
    return size // 2 + jnp.where(lax.rem(k, 2) == 1, -half, half)


def kernel(
    ny, nz, nt,
    x_hbm, w_hbm, a_hbm, l_hbm, r_hbm, s_hbm, returned, weight,
    x_v, w_v, s_v, perm_v, blocks, near, mixed,
    send1, owned, around, send2, recv2,
    load_sem, send_sem, recv_sem,
):
    face, tile = lax.axis_index("face"), lax.axis_index("tile")
    z, y = lax.div(face, ny), lax.rem(face, ny)
    faces, share, width = owned.shape
    points = faces * share
    depth = w_v.shape[1] // LOADS
    cuts = sorted({0, max(1, nz * 3 // 16), max(1, nz * 5 // 16), max(1, nz * 9 // 16), nz})
    groups = list(zip(cuts[:-1], cuts[1:]))

    def beside(d):
        return lax.rem(tile + nt + d, nt)

    def plane(k):
        return lax.rem(z + away(k, nz), nz)

    def to_mates(act, first=0, last=faces - 1):
        def step(i, carry):
            act(plane(lax.div(i, ny)) * ny + lax.rem(y + away(lax.rem(i, ny), ny), ny))
            return carry

        lax.fori_loop(first, last, step, 0)

    loads = []
    for c in range(LOADS):
        span = pl.ds(c * depth, depth)
        loads.append(pltpu.make_async_copy(x_hbm.at[span], x_v.at[span], load_sem.at[2 * c]))
        loads.append(pltpu.make_async_copy(w_hbm.at[:, span], w_v.at[:, span], load_sem.at[2 * c + 1]))
    for copy in loads:
        copy.start()

    barrier = pltpu.get_barrier_semaphore()
    to_mates(lambda m: pl.semaphore_signal(barrier, inc=1, device_id={"face": m}, device_id_type=MESH))
    for d in OTHERS:
        pl.semaphore_signal(barrier, inc=1, device_id={"tile": beside(d)}, device_id_type=MESH)

    for i, (src, dst) in enumerate((
        (s_hbm, s_v), (a_hbm, blocks.at[0]), (l_hbm, blocks.at[1]), (r_hbm, blocks.at[2])
    )):
        loads.append(pltpu.make_async_copy(src, dst, load_sem.at[2 * LOADS + i]))
        loads[-1].start()

    total = None
    for c in range(LOADS):
        span = pl.ds(c * depth, depth)
        loads[2 * c].wait()
        loads[2 * c + 1].wait()
        term = dot(w_v[:, span], x_v[span, :])
        total = term if total is None else total + term
    loads[2 * LOADS].wait()
    rows = lax.broadcasted_iota(jnp.int32, (points, points), 0)
    perm_v[...] = jnp.where(rows == s_v[...], 1.0, 0.0).astype(BF16)
    send1[...] = dot(perm_v[...], total.astype(BF16), 0, 0).astype(BF16).reshape(faces, share, width)
    owned[face] = send1[face]
    for copy in loads[2 * LOADS + 1:]:
        copy.wait()

    pl.semaphore_wait(barrier, faces - 1 + len(OTHERS))

    def remote(src, dst, phase, other):
        return pltpu.make_async_remote_copy(
            src_ref=src, dst_ref=dst, send_sem=send_sem.at[phase], recv_sem=recv_sem.at[phase],
            device_id=other, device_id_type=MESH,
        )

    def exchange(phase, src, dst, first, last):
        to_mates(lambda m: remote(src.at[m], dst.at[face], phase, {"face": m}).start(), first, last)
        span = pl.ds(0, last - first)
        return remote(src.at[span], dst.at[span], phase, {"face": lax.rem(face + 1, faces)})

    parts = [
        exchange(9 + i, send1, owned, first * ny, min(last * ny, faces - 1))
        for i, (first, last) in enumerate(groups)
    ]
    to_prev = remote(blocks, near.at[1], 2, {"tile": beside(-1)})
    to_next = remote(blocks, near.at[0], 3, {"tile": beside(1)})
    to_prev.start()
    to_next.start()
    waits = parts + [to_prev, to_next]
    weight[...] = dot(w_v[...], perm_v[...], 0, 0).astype(BF16)

    def hand_on(first, last):
        def step(k, carry):
            span = pl.ds(plane(k) * ny, ny)
            for j in (2, 3, 0, 1):
                remote(owned.at[span], around.at[j, span], 4 + j, {"tile": beside(-OTHERS[j])}).start()
            return carry

        lax.fori_loop(first, last, step, 0)

    for part, (first, last) in reversed(list(zip(parts, groups))):
        part.wait_recv()
        hand_on(first, last)
    fields = [remote(owned, around.at[j], 4 + j, {"tile": beside(-d)}) for j, d in enumerate(OTHERS)]
    waits += fields

    to_prev.wait_recv()
    to_next.wait_recv()
    a, l, r = (blocks[i] for i in range(3))
    ap, lp, rp = (near[0, i] for i in range(3))
    an, ln, rn = (near[1, i] for i in range(3))
    mixed[0] = (dot(a, a, 0, 0) + dot(ln, ln, 0, 0) + dot(rp, rp, 0, 0)).astype(BF16)
    mixed[1] = (dot(a, r, 0, 0) + dot(ln, an, 0, 0)).astype(BF16)
    mixed[2] = (dot(a, l, 0, 0) + dot(rp, ap, 0, 0)).astype(BF16)
    mixed[3] = dot(ln, rn, 0, 0).astype(BF16)
    mixed[4] = dot(rp, lp, 0, 0).astype(BF16)
    adjoint = dot(mixed[0], owned[...].reshape(points, width))
    for j, field in enumerate(fields):
        field.wait_recv()
        adjoint = adjoint + dot(mixed[1 + j], around[j].reshape(points, width))
    send2[...] = adjoint.astype(BF16).reshape(faces, share, width)

    waits.append(exchange(8, send2, recv2, 0, faces - 1))
    recv2[face] = send2[face]
    waits[-1].wait_recv()
    returned[...] = recv2[...].reshape(points, width)
    for wait in waits:
        wait.wait_send()


def spread(weight_ref, returned_ref, out_hbm, out_v, out_sem):
    depth = weight_ref.shape[0] // STORES
    stores = []
    for c in range(STORES):
        span = pl.ds(c * depth, depth)
        out_v[span, :] = dot(weight_ref[span, :], returned_ref[...]).astype(BF16)
        stores.append(pltpu.make_async_copy(out_v.at[span], out_hbm.at[span], out_sem.at[c]))
        stores[-1].start()
    for store in stores:
        store.wait()


def solution(mesh):
    nf, nt = mesh.shape["face"], mesh.shape["tile"]
    ny = 8 if nf == 128 else 2
    nz = nf // ny

    def local(model_field, interp_weight, center_block, lower_block, upper_block, owner_slots):
        model, width = model_field.shape
        points = interp_weight.shape[0]
        field = pltpu.VMEM((nf, points // nf, width), BF16)
        returned, weight = pl.pallas_call(
            functools.partial(kernel, ny, nz, nt),
            out_shape=(
                jax.ShapeDtypeStruct((points, width), BF16),
                jax.ShapeDtypeStruct((model, points), BF16),
            ),
            in_specs=[pl.BlockSpec(memory_space=pltpu.HBM)] * 6,
            out_specs=[pl.BlockSpec(memory_space=pltpu.VMEM)] * 2,
            scratch_shapes=[
                pltpu.VMEM((model, width), BF16),
                pltpu.VMEM((points, model), BF16),
                pltpu.VMEM((1, points), jnp.int32),
                pltpu.VMEM((points, points), BF16),
                pltpu.VMEM((3, points, points), BF16),
                pltpu.VMEM((2, 3, points, points), BF16),
                pltpu.VMEM((5, points, points), BF16),
                field, field, pltpu.VMEM((4, nf, points // nf, width), BF16), field, field,
                pltpu.SemaphoreType.DMA((4 + 2 * LOADS,)),
                pltpu.SemaphoreType.DMA((13,)),
                pltpu.SemaphoreType.DMA((13,)),
            ],
            compiler_params=pltpu.CompilerParams(
                collective_id=0, has_side_effects=True, vmem_limit_bytes=16 * 2**20
            ),
            cost_estimate=pl.CostEstimate(
                flops=6 * points * model * width, bytes_accessed=6 * model * points, transcendentals=0
            ),
        )(*(pltpu.with_memory_space_constraint(v, pltpu.HBM) for v in (
            model_field, interp_weight, center_block, lower_block, upper_block, owner_slots
        )))
        return pl.pallas_call(
            spread,
            out_shape=jax.ShapeDtypeStruct((model, width), BF16),
            in_specs=[pl.BlockSpec(memory_space=pltpu.VMEM)] * 2,
            out_specs=pl.BlockSpec(memory_space=pltpu.HBM),
            scratch_shapes=[pltpu.VMEM((model, width), BF16), pltpu.SemaphoreType.DMA((STORES,))],
            compiler_params=pltpu.CompilerParams(vmem_limit_bytes=16 * 2**20),
            cost_estimate=pl.CostEstimate(
                flops=2 * points * model * width, bytes_accessed=4 * model * points, transcendentals=0
            ),
        )(weight, returned)

    placed = P(("face", "tile"), None)
    return jax.shard_map(
        local, mesh=mesh, in_specs=(placed,) * 6, out_specs=placed, check_vma=False
    )
```
